32 devices in a mesh: face: 4 (over y, x), inface: 8 (over z, core).
Axes of the slice: x: 2, y: 2, z: 4, core: 2. Of those that a mesh axis runs over, the one named last changes fastest.
Arguments:
- model_state: float32 [4, 58, 131072], P(None, None, ('face', 'inface')), may hold values from -6 to 6
- coupling: float32 [58, 131072], P(None, ('face', 'inface')), may hold values from 0.05 to 20
- cosine: float32 [131072], P(('face', 'inface')), may hold values from 0.15 to 1
- albedo: float32 [131072], P(('face', 'inface')), may hold values from 0.05 to 0.8
- absorb: float32 [14], replicated, may hold values from 0.005 to 0.5
- weights: float32 [14], replicated, may hold values from 0.2 to 1.5
- span_map: int32 [4, 256], P('face', 'inface'), may hold values from 0 to 255, as said below
- sunlit: int32 [4, 256], P('face', 'inface'), may hold values from 0 to 1, as said below
Outputs:
- new_state: float32 [4, 58, 131072], P(None, None, ('face', 'inface'))
- surface_flux: float32 [131072], P(('face', 'inface'))
The draws below stay inside these ranges and needn't reach their ends.
Inputs may be any that keep to these rules, and one draw needn't show every extreme that they name: `span_map`: in each face block the entries are a permutation of the spans; the blocks of one device go to each device of its face block exactly 4 at a time. The sunlit spans of a device and those of the device whose face index differs in bit 1 (same inface index) number 32 together; a device holds at most 28 sunlit spans, and some device exactly 28.
All inputs are finite; a program needn't handle non-finite values.
Results may differ from the reference program's by a relative error of at most 0.000023.
Values sent between devices are 32-bit elements; how exact they have to be, the bound alone decides.
A program may use at most 64 MiB of HBM per device.

```python
import math
import jax
import jax.numpy as jnp
from jax import lax

LEV = 58
NB = 14
FIELDS = 4
PCOLS = 128
BLK_DEV = 32
SUN_MAX = 28
BLKS_FACE = 256
COLS = 131072
N_FACE = 4
N_INFACE = 8


def draw_span_map(key, part):
    inface_count = BLKS_FACE // BLK_DEV
    per_owner = BLK_DEV // inface_count
    source_keys = jax.random.split(jax.random.fold_in(key, 11), N_FACE * inface_count)
    target_keys = jax.random.split(jax.random.fold_in(key, 23), N_FACE * inface_count)
    source_perm = jax.vmap(lambda k: jax.random.permutation(k, BLK_DEV))(source_keys).reshape(N_FACE, inface_count, BLK_DEV)
    target_perm = jax.vmap(lambda k: jax.random.permutation(k, BLK_DEV))(target_keys).reshape(N_FACE, inface_count, BLK_DEV)
    owner = source_perm // per_owner
    within = source_perm % per_owner
    face_index = jnp.arange(N_FACE)[:, None, None]
    source_index = jnp.arange(inface_count)[None, :, None]
    slot = target_perm[face_index, owner, source_index * per_owner + within]
    return (owner * BLK_DEV + slot).reshape(N_FACE, BLKS_FACE).astype(jnp.int32)


def draw_sunlit(key, part):
    inface_count = BLKS_FACE // BLK_DEV
    counts = jax.random.randint(jax.random.fold_in(key, 5), (2, inface_count), BLK_DEV - SUN_MAX, SUN_MAX + 1)
    chosen = jax.random.randint(jax.random.fold_in(key, 7), (), 0, 2 * inface_count)
    flat_counts = counts.reshape(-1)
    flat_counts = jnp.where(jnp.arange(2 * inface_count) == chosen, SUN_MAX, flat_counts)
    counts = flat_counts.reshape(2, inface_count)
    all_counts = jnp.concatenate([counts, BLK_DEV - counts], axis=0)
    perm_keys = jax.random.split(jax.random.fold_in(key, 9), N_FACE * inface_count)
    ranks = jax.vmap(lambda k: jax.random.permutation(k, BLK_DEV))(perm_keys).reshape(N_FACE, inface_count, BLK_DEV)
    flags = (ranks < all_counts[:, :, None]).astype(jnp.int32)
    return flags.reshape(N_FACE, BLKS_FACE)


def level_of(own_key, dims, pieces, low, largest):
    def one(dim, blocks):
        steps = jax.random.uniform(jax.random.fold_in(jax.random.fold_in(own_key, 6), dim), (blocks,), jnp.float32, low / len(pieces), largest / len(pieces))
        return jnp.repeat(jnp.exp(steps), dims[dim] // blocks).reshape((-1,) + (1,) * (len(dims) - dim - 1))

    level = one(*pieces[0])
    for cut in pieces[1:]:
        level = level * one(*cut)
    return level


def scatter_about(stream_key, shape, spread, reach, cuts=(), held_as=jnp.bfloat16):
    level = level_of(stream_key, shape, cuts, -0.22, 0.18) if cuts else 1.0
    array = jax.random.normal(stream_key, shape, jnp.float32) * spread * level
    return jnp.minimum(jnp.maximum(array, -reach), reach).astype(held_as)


def setup_inputs(seed: int = 0) -> dict:
    keys = jax.random.split(jax.random.key(seed), 9)
    model_state = scatter_about(keys[0], (FIELDS, LEV, COLS), 1.0, 6.0, ((2, 32),), jnp.float32)
    coupling = jnp.clip(jnp.exp(math.log(20.0) - 5.9914645 * jax.random.uniform(keys[1], (LEV, COLS), jnp.float32) ** level_of(keys[1], (LEV, COLS), ((1, 32),), -0.2, 0.2)), 0.05, 20.0)
    cosine = jnp.clip(0.15 + 0.85 * jax.random.uniform(keys[2], (COLS,), jnp.float32) ** level_of(keys[2], (COLS,), ((0, 32),), -0.2, 0.2), 0.15, 1.0)
    albedo = jnp.clip(0.05 + 0.75 * jax.random.uniform(keys[3], (COLS,), jnp.float32) ** level_of(keys[3], (COLS,), ((0, 32),), -0.2, 0.2), 0.05, 0.8)
    absorb = jnp.clip(jnp.exp(jax.random.uniform(keys[4], (NB,), jnp.float32, math.log(0.005), math.log(0.5))), 0.005, 0.5)
    weights = jnp.clip(jnp.exp(jax.random.uniform(keys[5], (NB,), jnp.float32, math.log(0.2), math.log(1.5))), 0.2, 1.5)
    span_map = draw_span_map(jax.random.fold_in(keys[8], 71), 0)
    sunlit = draw_sunlit(jax.random.fold_in(keys[8], 71), 0)
    return dict(model_state=model_state, coupling=coupling, cosine=cosine, albedo=albedo, absorb=absorb, weights=weights, span_map=span_map, sunlit=sunlit)


def vertical_solve(source_rows, coupling):
    levels = source_rows.shape[1]
    gains = []
    partial_values = []
    for level_index in range(levels):
        below = coupling[level_index]
        if level_index == 0:
            divisor = 1.0 + below
            current = source_rows[:, 0]
        else:
            above = coupling[level_index - 1]
            divisor = 1.0 + below + above - above * gains[-1]
            current = source_rows[:, level_index] + above * partial_values[-1]
        gains.append(below / divisor)
        partial_values.append(current / divisor)
    solved = [partial_values[-1]]
    for level_index in range(levels - 2, -1, -1):
        solved.append(partial_values[level_index] + gains[level_index] * solved[-1])
    return jnp.stack(solved[::-1], axis=1)


def two_stream(moisture, cosine, albedo, absorb, weights):
    levels = moisture.shape[0]
    down_flux = [weights[:, None] * cosine[None, :]]
    transmit = []
    reflect = []
    for level_index in range(levels):
        optical = absorb[:, None] * (1.2 + jnp.tanh(moisture[level_index]))[None, :]
        passed = jnp.exp(-optical / cosine[None, :])
        transmit.append(passed)
        reflect.append(0.3 * (1.0 - passed))
        down_flux.append(down_flux[-1] * passed)
    up_flux = [None] * (levels + 1)
    up_flux[levels] = albedo[None, :] * down_flux[levels]
    for level_index in range(levels - 1, -1, -1):
        up_flux[level_index] = up_flux[level_index + 1] * transmit[level_index] + reflect[level_index] * down_flux[level_index]
    heating = jnp.stack([5.0 * jnp.sum(down_flux[k] - down_flux[k + 1] + up_flux[k + 1] - up_flux[k], axis=0) for k in range(levels)], axis=0)
    surface = jnp.sum((1.0 - albedo)[None, :] * down_flux[levels], axis=0)
    return heating, surface


def reference(model_state, coupling, cosine, albedo, absorb, weights, span_map, sunlit):
    groups = N_FACE * N_INFACE
    columns = BLK_DEV * PCOLS
    grouped_state = model_state.reshape(FIELDS, LEV, groups, columns).transpose(2, 0, 1, 3)
    grouped_coupling = coupling.reshape(LEV, groups, columns).transpose(1, 0, 2)

    def solve_group(operands):
        return vertical_solve(operands[0], operands[1])

    diffused = lax.map(solve_group, (grouped_state, grouped_coupling))
    diffused = diffused.transpose(1, 2, 0, 3).reshape(FIELDS, LEV, N_FACE, BLKS_FACE, PCOLS)
    face_rows = jnp.arange(N_FACE)[:, None]
    moisture = jnp.zeros((LEV, N_FACE, BLKS_FACE, PCOLS), jnp.float32).at[:, face_rows, span_map].set(diffused[1])
    grouped_moisture = moisture.reshape(LEV, groups, columns).transpose(1, 0, 2)

    def radiate_group(operands):
        return two_stream(operands[0], operands[1], operands[2], absorb, weights)

    heating, surface = lax.map(radiate_group, (grouped_moisture, cosine.reshape(groups, columns), albedo.reshape(groups, columns)))
    flags = jnp.repeat(sunlit.astype(jnp.float32), PCOLS, axis=1).reshape(groups, columns)
    heating = heating * flags[:, None, :]
    surface = surface * flags
    heating = heating.transpose(1, 0, 2).reshape(LEV, N_FACE, BLKS_FACE, PCOLS)
    heating_home = heating[:, face_rows, span_map]
    new_state = diffused.at[0].add(heating_home)
    return new_state.reshape(FIELDS, LEV, COLS), surface.reshape(COLS)
```

```python
import functools
import math

import jax
import jax.numpy as jnp
from jax import lax
from jax.experimental import pallas as pl
from jax.experimental.pallas import tpu as pltpu
from jax.sharding import PartitionSpec as P

MESH = pl.DeviceIdType.MESH
LANES = 128


def exchange(count, axis, source, target, send_sem, recv_sem):
    me = lax.axis_index(axis)
    copies = []
    for k in range(1, count):
        peer = lax.rem(me + k, count)
        copy = pltpu.make_async_remote_copy(
            src_ref=source,
            dst_ref=target.at[me],
            send_sem=send_sem.at[k],
            recv_sem=recv_sem.at[k],
            device_id={axis: peer},
            device_id_type=MESH,
        )
        copy.start()
        copies.append(copy)
    return copies


def finish(count, axis, source, target, send_sem, recv_sem, copies):
    me = lax.axis_index(axis)
    for k in range(1, count):
        origin = lax.rem(me + count - k, count)
        pltpu.make_async_remote_copy(
            src_ref=source,
            dst_ref=target.at[origin],
            send_sem=send_sem.at[k],
            recv_sem=recv_sem.at[k],
            device_id={axis: origin},
            device_id_type=MESH,
        ).wait_recv()
    for copy in copies:
        copy.wait_send()


def greet(count, axis):
    me = lax.axis_index(axis)
    barrier = pltpu.get_barrier_semaphore()
    for k in range(1, count):
        pl.semaphore_signal(barrier, inc=1, device_id={axis: lax.rem(me + k, count)}, device_id_type=MESH)
    pl.semaphore_wait(barrier, count - 1)


def sky_kernel(count, spans, cosine, albedo, sunlit, span_map, gathered, packed, send_sem, recv_sem):
    me = lax.axis_index("inface")
    for s in range(spans):
        packed[pl.ds(s, 1), :] = cosine[pl.ds(s, 1), :] * sunlit[0, s].astype(jnp.float32)
    packed[pl.ds(spans, spans), :] = albedo[...]
    packed[pl.ds(2 * spans, 8), :] = jnp.full((8, LANES), -1.0, jnp.float32)
    packed[pl.ds(2 * spans, 1), pl.ds(0, spans)] = span_map[...].astype(jnp.float32)
    gathered[me] = packed[...]
    greet(count, "inface")
    copies = exchange(count, "inface", packed, gathered, send_sem, recv_sem)
    finish(count, "inface", packed, gathered, send_sem, recv_sem, copies)


def gather_sky(count, cosine, albedo, sunlit, span_map):
    spans = sunlit.shape[1]
    rows = 2 * spans + 8
    return pl.pallas_call(
        functools.partial(sky_kernel, count, spans),
        out_shape=jax.ShapeDtypeStruct((count, rows, LANES), jnp.float32),
        in_specs=[
            pl.BlockSpec(memory_space=pltpu.VMEM),
            pl.BlockSpec(memory_space=pltpu.VMEM),
            pl.BlockSpec(memory_space=pltpu.SMEM),
            pl.BlockSpec(memory_space=pltpu.VMEM),
        ],
        out_specs=pl.BlockSpec(memory_space=pltpu.VMEM),
        scratch_shapes=[
            pltpu.VMEM((rows, LANES), jnp.float32),
            pltpu.SemaphoreType.DMA((count,)),
            pltpu.SemaphoreType.DMA((count,)),
        ],
        compiler_params=pltpu.CompilerParams(collective_id=0, has_side_effects=True),
        name="gather_sky",
    )(cosine, albedo, sunlit, span_map)


def flux_kernel(count, spans, flux, sky, result, gathered, send_sem, recv_sem):
    me = lax.axis_index("inface")
    gathered[me] = flux[...]
    greet(count, "inface")
    copies = exchange(count, "inface", flux, gathered, send_sem, recv_sem)
    finish(count, "inface", flux, gathered, send_sem, recv_sem, copies)
    mine = (lax.broadcasted_iota(jnp.int32, (spans, spans), 0) + me * spans).astype(jnp.float32)
    total = jnp.zeros((spans, LANES), jnp.float32)
    for r in range(count):
        span_of = sky[r, pl.ds(2 * spans, 1), pl.ds(0, spans)]
        pick = jnp.where(mine == span_of, 1.0, 0.0)
        total = total + jnp.dot(
            pick, gathered[r], preferred_element_type=jnp.float32, precision=lax.Precision.HIGHEST
        )
    result[...] = total


def scatter_flux(count, flux, sky):
    spans = flux.shape[0]
    return pl.pallas_call(
        functools.partial(flux_kernel, count, spans),
        out_shape=jax.ShapeDtypeStruct(flux.shape, jnp.float32),
        in_specs=[pl.BlockSpec(memory_space=pltpu.VMEM)] * 2,
        out_specs=pl.BlockSpec(memory_space=pltpu.VMEM),
        scratch_shapes=[
            pltpu.VMEM((count, spans, LANES), jnp.float32),
            pltpu.SemaphoreType.DMA((count,)),
            pltpu.SemaphoreType.DMA((count,)),
        ],
        compiler_params=pltpu.CompilerParams(collective_id=1, has_side_effects=True),
        name="scatter_flux",
    )(flux, sky)


def column_kernel(
    span_map, absorb, weights, sky, state_in, coupling_in, state_out, flux, state, coupling, gain, depth, path,
    sun, in_sem, out_sem,
):
    fields, levels, blocks, _ = state.shape
    bands = absorb.shape[0]

    def columns(c):
        return pl.ds(c * LANES, LANES)

    for c in range(blocks):
        pltpu.make_async_copy(coupling_in.at[:, columns(c)], coupling.at[:, c, :], in_sem.at[0]).start()
        pltpu.make_async_copy(state_in.at[:, :, columns(c)], state.at[:, :, c, :], in_sem.at[1]).start()

    for e in range(blocks):
        span = span_map[0, e]
        owner, slot = span // blocks, span % blocks
        sun[0, pl.ds(e, 1), :] = sky[owner, pl.ds(slot, 1), :]
        sun[1, pl.ds(e, 1), :] = sky[owner, pl.ds(slot + blocks, 1), :]

    pltpu.make_async_copy(coupling, coupling, in_sem.at[0]).wait()
    pltpu.make_async_copy(state, state, in_sem.at[1]).wait()

    below = coupling[0]
    scale = 1.0 / (1.0 + below)
    gain_now = below * scale
    gain[0] = gain_now
    values = []
    for f in range(fields):
        value = state[f, 0] * scale
        state[f, 0] = value
        values.append(value)

    def eliminate(l, carry):
        above, gain_last, *last = carry
        below = coupling[l]
        scale = 1.0 / (1.0 + below + above - above * gain_last)
        gain_now = below * scale
        gain[l] = gain_now
        now = []
        for f in range(fields):
            value = (state[f, l] + above * last[f]) * scale
            state[f, l] = value
            now.append(value)
        return (below, gain_now, *now)

    carry = lax.fori_loop(1, levels, eliminate, (below, gain_now, *values), unroll=3)

    def substitute(k, carry):
        l = levels - 2 - k
        g = gain[l]
        now = []
        for f in range(fields):
            value = state[f, l] + g * carry[f]
            state[f, l] = value
            now.append(value)
        return tuple(now)

    lax.fori_loop(0, levels - 1, substitute, tuple(carry[2:]), unroll=3)

    for c in range(blocks):
        pltpu.make_async_copy(
            state.at[pl.ds(1, fields - 1), :, c, :], state_out.at[pl.ds(1, fields - 1), :, columns(c)], out_sem.at[0]
        ).start()

    cosine = sun[0]
    lit = cosine > 0.0
    slant = (-math.log2(math.e)) / jnp.where(lit, cosine, 1.0)

    def optics(l, total):
        step = (1.2 + jnp.tanh(state[1, l])) * slant
        depth[l] = step
        path[l] = total
        return total + step

    whole = lax.fori_loop(0, levels, optics, jnp.zeros_like(slant), unroll=2)
    path[levels] = whole

    for g in range(blocks // 8):
        rows = pl.ds(g * 8, 8)
        shape = (8, LANES)
        coefficient = [jnp.full(shape, absorb[b], jnp.float32) for b in range(bands)]
        weight = [jnp.full(shape, 0.3 * weights[b], jnp.float32) for b in range(bands)]
        surface = sun[1, rows, :]
        sun_rows = sun[0, rows, :]
        bottom = path[levels, rows, :]
        ups = []
        sum_up = jnp.zeros(shape, jnp.float32)
        sum_down = jnp.zeros(shape, jnp.float32)
        for b in range(bands):
            down = weight[b] * jnp.exp2(coefficient[b] * bottom)
            up = surface * (down * (1.0 / 0.3))
            ups.append(up)
            sum_up = sum_up + up
            sum_down = sum_down + down
        flux[rows, :] = (1.0 - surface) * sun_rows * (sum_down * (1.0 / 0.3))
        net = sum_up - sum_down * (1.0 / 0.3)
        factor = 5.0 * sun_rows

        def radiate(k, carry):
            l = levels - 1 - k
            net_below, *ups = carry
            step = depth[l, rows, :]
            above = path[l, rows, :]
            sum_up = [None, None]
            sum_down = [None, None]
            now = []
            for b in range(bands):
                passed = jnp.exp2(coefficient[b] * step)
                down = weight[b] * jnp.exp2(coefficient[b] * above)
                up = (ups[b] - down) * passed + down
                now.append(up)
                h = b % 2
                sum_up[h] = up if sum_up[h] is None else sum_up[h] + up
                sum_down[h] = down if sum_down[h] is None else sum_down[h] + down
            net = (sum_up[0] + sum_up[1]) - (sum_down[0] + sum_down[1]) * (1.0 / 0.3)
            state[0, l, rows, :] = state[0, l, rows, :] + factor * (net_below - net)
            return (net, *now)

        lax.fori_loop(0, levels, radiate, (net, *ups), unroll=2)
        for c in range(g * 8, g * 8 + 8):
            pltpu.make_async_copy(state.at[0, :, c, :], state_out.at[0, :, columns(c)], out_sem.at[1]).start()

    pltpu.make_async_copy(state.at[pl.ds(1, fields - 1)], state.at[pl.ds(1, fields - 1)], out_sem.at[0]).wait()
    pltpu.make_async_copy(state.at[0], state.at[0], out_sem.at[1]).wait()


def run_columns(span_map, absorb, weights, sky, model_state, coupling):
    fields, levels, columns = model_state.shape
    blocks = columns // LANES
    smem = pl.BlockSpec(memory_space=pltpu.SMEM)
    return pl.pallas_call(
        column_kernel,
        out_shape=(
            jax.ShapeDtypeStruct(model_state.shape, jnp.float32),
            jax.ShapeDtypeStruct((blocks, LANES), jnp.float32),
        ),
        in_specs=[
            smem,
            smem,
            smem,
            pl.BlockSpec(memory_space=pltpu.VMEM),
            pl.BlockSpec(memory_space=pl.ANY),
            pl.BlockSpec(memory_space=pl.ANY),
        ],
        out_specs=(pl.BlockSpec(memory_space=pl.ANY), pl.BlockSpec(memory_space=pltpu.VMEM)),
        scratch_shapes=[
            pltpu.VMEM((fields, levels, blocks, LANES), jnp.float32),
            pltpu.VMEM((levels, blocks, LANES), jnp.float32),
            pltpu.VMEM((levels, blocks, LANES), jnp.float32),
            pltpu.VMEM((levels, blocks, LANES), jnp.float32),
            pltpu.VMEM((levels + 1, blocks, LANES), jnp.float32),
            pltpu.VMEM((2, blocks, LANES), jnp.float32),
            pltpu.SemaphoreType.DMA((2,)),
            pltpu.SemaphoreType.DMA((2,)),
        ],
        compiler_params=pltpu.CompilerParams(vmem_limit_bytes=24 * 1024 * 1024),
        name="columns",
    )(span_map, absorb, weights, sky, model_state, coupling)


def body(model_state, coupling, cosine, albedo, absorb, weights, span_map, sunlit):
    count = lax.axis_size("inface")
    spans = span_map.shape[1]
    sky = gather_sky(count, cosine.reshape(spans, LANES), albedo.reshape(spans, LANES), sunlit, span_map)
    new_state, flux = run_columns(span_map, absorb, weights, sky, model_state, coupling)
    surface = scatter_flux(count, flux, sky)
    return new_state, surface.reshape(cosine.shape)


def solution(mesh):
    in_specs = (
        P(None, None, ("face", "inface")),
        P(None, ("face", "inface")),
        P(("face", "inface")),
        P(("face", "inface")),
        P(),
        P(),
        P("face", "inface"),
        P("face", "inface"),
    )
    out_specs = (P(None, None, ("face", "inface")), P(("face", "inface")))
    return jax.shard_map(body, mesh=mesh, in_specs=in_specs, out_specs=out_specs, check_vma=False)
```

```python
import functools
import math

import jax
import jax.numpy as jnp
from jax import lax
from jax.experimental import pallas as pl
from jax.experimental.pallas import tpu as pltpu
from jax.sharding import PartitionSpec as P

MESH = pl.DeviceIdType.MESH
LANES = 128


def exchange(count, axis, source, target, send_sem, recv_sem):
    me = lax.axis_index(axis)
    copies = []
    for k in range(1, count):
        peer = lax.rem(me + k, count)
        copy = pltpu.make_async_remote_copy(
            src_ref=source,
            dst_ref=target.at[me],
            send_sem=send_sem.at[k],
            recv_sem=recv_sem.at[k],
            device_id={axis: peer},
            device_id_type=MESH,
        )
        copy.start()
        copies.append(copy)
    return copies


def finish(count, axis, source, target, send_sem, recv_sem, copies):
    me = lax.axis_index(axis)
    for k in range(1, count):
        origin = lax.rem(me + count - k, count)
        pltpu.make_async_remote_copy(
            src_ref=source,
            dst_ref=target.at[origin],
            send_sem=send_sem.at[k],
            recv_sem=recv_sem.at[k],
            device_id={axis: origin},
            device_id_type=MESH,
        ).wait_recv()
    for copy in copies:
        copy.wait_send()


def greet(count, axis):
    me = lax.axis_index(axis)
    barrier = pltpu.get_barrier_semaphore()
    for k in range(1, count):
        pl.semaphore_signal(barrier, inc=1, device_id={axis: lax.rem(me + k, count)}, device_id_type=MESH)
    pl.semaphore_wait(barrier, count - 1)


SKIP = ()


def step_kernel(
    count, cosine, albedo, sunlit, span_map, span_row, absorb, weights, state_in, coupling_in, state_out, surface_out,
    state, partial, coupling, gain, depth, path, sun, packed, sky, flux, fluxes, in_sem, out_sem, send_sem, recv_sem,
):
    fields, levels, blocks, _ = partial.shape
    bands = absorb.shape[0]
    me = lax.axis_index("inface") if count > 1 else 0

    def columns(c):
        return pl.ds(c * LANES, LANES)

    def field(f, first=0, size=blocks):
        return pl.ds(first * fields + f, size, stride=fields)

    for c in range(blocks):
        pltpu.make_async_copy(coupling_in.at[:, columns(c)], coupling.at[:, c, :], in_sem.at[0]).start()
    for c in range(blocks):
        pltpu.make_async_copy(state_in.at[:, :, columns(c)], state.at[:, pl.ds(c * fields, fields), :], in_sem.at[1]).start()

    for s in range(blocks):
        packed[pl.ds(s, 1), :] = cosine[pl.ds(s, 1), :] * sunlit[0, s].astype(jnp.float32)
    packed[pl.ds(blocks, blocks), :] = albedo[...]
    packed[pl.ds(2 * blocks, 8), :] = jnp.full((8, LANES), -1.0, jnp.float32)
    packed[pl.ds(2 * blocks, 1), pl.ds(0, blocks)] = span_row[...].astype(jnp.float32)
    sky[me] = packed[...]
    if count > 1:
        greet(count, "inface")
    sky_copies = exchange(count, "inface", packed, sky, send_sem.at[0], recv_sem.at[0]) if count > 1 else []

    pltpu.make_async_copy(coupling, coupling, in_sem.at[0]).wait()
    pltpu.make_async_copy(state, state, in_sem.at[1]).wait()

    if "solve" not in SKIP:
        below = coupling[0]
        scale = 1.0 / (1.0 + below)
        gain_now = below * scale
        gain[0] = gain_now
        values = []
        for f in range(fields):
            value = state[0, field(f), :] * scale
            partial[f, 0] = value
            values.append(value)

        def eliminate(l, carry):
            above, gain_last, *last = carry
            below = coupling[l]
            scale = 1.0 / (1.0 + below + above - above * gain_last)
            gain_now = below * scale
            gain[l] = gain_now
            now = []
            for f in range(fields):
                value = (state[l, field(f), :] + above * last[f]) * scale
                partial[f, l] = value
                now.append(value)
            return (below, gain_now, *now)

        carry = lax.fori_loop(1, levels, eliminate, (below, gain_now, *values), unroll=3)
        for f in range(fields):
            state[levels - 1, field(f), :] = carry[2 + f]

        def substitute(k, carry):
            l = levels - 2 - k
            g = gain[l]
            now = []
            for f in range(fields):
                value = partial[f, l] + g * carry[f]
                state[l, field(f), :] = value
                now.append(value)
            return tuple(now)

        lax.fori_loop(0, levels - 1, substitute, tuple(carry[2:]), unroll=3)

    if count > 1:
        finish(count, "inface", packed, sky, send_sem.at[0], recv_sem.at[0], sky_copies)
    for e in range(blocks):
        span = span_map[0, e]
        owner, slot = span // blocks, span % blocks
        sun[0, pl.ds(e, 1), :] = sky[owner, pl.ds(slot, 1), :]
        sun[1, pl.ds(e, 1), :] = sky[owner, pl.ds(slot + blocks, 1), :]

    cosine_here = sun[0]
    slant = (-math.log2(math.e)) / jnp.where(cosine_here > 0.0, cosine_here, 1.0)

    def optics(l, total):
        step = (1.2 + jnp.tanh(state[l, field(1), :])) * slant
        depth[l] = step
        path[l] = total
        return total + step

    if "optics" not in SKIP:
        bottom = lax.fori_loop(0, levels, optics, jnp.zeros_like(slant), unroll=2)
        path[levels] = bottom
    else:
        bottom = slant

    shape = (8, LANES)
    for g in range(blocks // 8):
        rows = pl.ds(g * 8, 8)
        total = jnp.zeros(shape, jnp.float32)
        for b in range(bands):
            total = total + weights[b] * jnp.exp2(absorb[b] * path[levels, rows, :])
        flux[rows, :] = (1.0 - sun[1, rows, :]) * sun[0, rows, :] * total
    fluxes[me] = flux[...]
    flux_copies = exchange(count, "inface", flux, fluxes, send_sem.at[1], recv_sem.at[1]) if count > 1 else []

    for g in range(blocks // 8):
        rows = pl.ds(g * 8, 8)
        coefficient = [jnp.full(shape, absorb[b], jnp.float32) for b in range(bands)]
        weight = [jnp.full(shape, 0.3 * weights[b], jnp.float32) for b in range(bands)]
        reflected = sun[1, rows, :] * (1.0 / 0.3)
        low = path[levels, rows, :]
        ups = []
        sum_up = jnp.zeros(shape, jnp.float32)
        sum_down = jnp.zeros(shape, jnp.float32)
        for b in range(bands):
            down = weight[b] * jnp.exp2(coefficient[b] * low)
            up = reflected * down
            ups.append(up)
            sum_up = sum_up + up
            sum_down = sum_down + down
        net = sum_up - sum_down * (1.0 / 0.3)
        factor = 5.0 * sun[0, rows, :]

        def radiate(k, carry):
            l = levels - 1 - k
            net_below, *ups = carry
            step = depth[l, rows, :]
            above = path[l, rows, :]
            sum_up = [None, None]
            sum_down = [None, None]
            now = []
            for b in range(bands):
                passed = jnp.exp2(coefficient[b] * step)
                down = weight[b] * jnp.exp2(coefficient[b] * above)
                up = (ups[b] - down) * passed + down
                now.append(up)
                h = b % 2
                sum_up[h] = up if sum_up[h] is None else sum_up[h] + up
                sum_down[h] = down if sum_down[h] is None else sum_down[h] + down
            net = (sum_up[0] + sum_up[1]) - (sum_down[0] + sum_down[1]) * (1.0 / 0.3)
            here = field(0, g * 8, 8)
            state[l, here, :] = state[l, here, :] + factor * (net_below - net)
            return (net, *now)

        if "radiate" not in SKIP:
            lax.fori_loop(0, levels, radiate, (net, *ups), unroll=2)
        for c in range(g * 8, g * 8 + 8):
            pltpu.make_async_copy(state.at[:, pl.ds(c * fields, fields), :], state_out.at[:, :, columns(c)], out_sem.at[0]).start()

    if count > 1:
        finish(count, "inface", flux, fluxes, send_sem.at[1], recv_sem.at[1], flux_copies)
    mine = (lax.broadcasted_iota(jnp.int32, (blocks, blocks), 0) + me * blocks).astype(jnp.float32)
    surface = jnp.zeros((blocks, LANES), jnp.float32)
    for r in range(count):
        span_of = sky[r, pl.ds(2 * blocks, 1), pl.ds(0, blocks)]
        pick = jnp.where(mine == span_of, 1.0, 0.0)
        surface = surface + jnp.dot(
            pick, fluxes[r], preferred_element_type=jnp.float32, precision=lax.Precision.HIGHEST
        )
    surface_out[...] = surface
    pltpu.make_async_copy(state, state, out_sem.at[0]).wait()


def run_step(count, cosine, albedo, sunlit, span_map, absorb, weights, model_state, coupling):
    levels, fields, columns = model_state.shape
    blocks = columns // LANES
    smem = pl.BlockSpec(memory_space=pltpu.SMEM)
    vmem = pl.BlockSpec(memory_space=pltpu.VMEM)
    anywhere = pl.BlockSpec(memory_space=pl.ANY)
    rows = 2 * blocks + 8
    return pl.pallas_call(
        functools.partial(step_kernel, count),
        out_shape=(
            jax.ShapeDtypeStruct(model_state.shape, jnp.float32),
            jax.ShapeDtypeStruct((blocks, LANES), jnp.float32),
        ),
        in_specs=[vmem, vmem, smem, smem, vmem, smem, smem, anywhere, anywhere],
        out_specs=(anywhere, vmem),
        scratch_shapes=[
            pltpu.VMEM((levels, blocks * fields, LANES), jnp.float32),
            pltpu.VMEM((fields, levels, blocks, LANES), jnp.float32),
            pltpu.VMEM((levels, blocks, LANES), jnp.float32),
            pltpu.VMEM((levels, blocks, LANES), jnp.float32),
            pltpu.VMEM((levels, blocks, LANES), jnp.float32),
            pltpu.VMEM((levels + 1, blocks, LANES), jnp.float32),
            pltpu.VMEM((2, blocks, LANES), jnp.float32),
            pltpu.VMEM((rows, LANES), jnp.float32),
            pltpu.VMEM((count, rows, LANES), jnp.float32),
            pltpu.VMEM((blocks, LANES), jnp.float32),
            pltpu.VMEM((count, blocks, LANES), jnp.float32),
            pltpu.SemaphoreType.DMA((2,)),
            pltpu.SemaphoreType.DMA((1,)),
            pltpu.SemaphoreType.DMA((2, max(count, 2))),
            pltpu.SemaphoreType.DMA((2, max(count, 2))),
        ],
        compiler_params=pltpu.CompilerParams(
            collective_id=0 if count > 1 else None, has_side_effects=True, vmem_limit_bytes=40 * 1024 * 1024
        ),
        name="step",
    )(cosine, albedo, sunlit, span_map, span_map, absorb, weights, model_state, coupling)


def body(model_state, coupling, cosine, albedo, absorb, weights, span_map, sunlit):
    count = lax.axis_size("inface")
    spans = span_map.shape[1]
    new_state, surface = run_step(
        count,
        cosine.reshape(spans, LANES),
        albedo.reshape(spans, LANES),
        sunlit,
        span_map,
        absorb,
        weights,
        model_state.transpose(1, 0, 2),
        coupling,
    )
    return new_state.transpose(1, 0, 2), surface.reshape(cosine.shape)


def solution(mesh):
    in_specs = (
        P(None, None, ("face", "inface")),
        P(None, ("face", "inface")),
        P(("face", "inface")),
        P(("face", "inface")),
        P(),
        P(),
        P("face", "inface"),
        P("face", "inface"),
    )
    out_specs = (P(None, None, ("face", "inface")), P(("face", "inface")))
    return jax.shard_map(body, mesh=mesh, in_specs=in_specs, out_specs=out_specs, check_vma=False)
```

```python
import functools
import math

import jax
import jax.numpy as jnp
from jax import lax
from jax.experimental import pallas as pl
from jax.experimental.pallas import tpu as pltpu
from jax.sharding import PartitionSpec as P

MESH = pl.DeviceIdType.MESH
LANES = 128


def exchange(count, axis, source, target, send_sem, recv_sem):
    me = lax.axis_index(axis)
    copies = []
    for k in range(1, count):
        peer = lax.rem(me + k, count)
        copy = pltpu.make_async_remote_copy(
            src_ref=source,
            dst_ref=target.at[me],
            send_sem=send_sem.at[k],
            recv_sem=recv_sem.at[k],
            device_id={axis: peer},
            device_id_type=MESH,
        )
        copy.start()
        copies.append(copy)
    return copies


def finish(count, axis, source, target, send_sem, recv_sem, copies):
    me = lax.axis_index(axis)
    for k in range(1, count):
        origin = lax.rem(me + count - k, count)
        pltpu.make_async_remote_copy(
            src_ref=source,
            dst_ref=target.at[origin],
            send_sem=send_sem.at[k],
            recv_sem=recv_sem.at[k],
            device_id={axis: origin},
            device_id_type=MESH,
        ).wait_recv()
    for copy in copies:
        copy.wait_send()


def greet(count, axis):
    me = lax.axis_index(axis)
    barrier = pltpu.get_barrier_semaphore()
    for k in range(1, count):
        pl.semaphore_signal(barrier, inc=1, device_id={axis: lax.rem(me + k, count)}, device_id_type=MESH)


def greeted(count):
    pl.semaphore_wait(pltpu.get_barrier_semaphore(), count - 1)


def sky_copy(axis, source, target, owner, peer, send_sem, recv_sem, k):
    return pltpu.make_async_remote_copy(
        src_ref=source,
        dst_ref=target.at[owner],
        send_sem=send_sem.at[k],
        recv_sem=recv_sem.at[k],
        device_id={axis: peer},
        device_id_type=MESH,
    )


SKIP = ()


def step_kernel(
    count, cosine_in, albedo_in, sunlit_in, span_map_in, absorb_in, weights_in, state_in, coupling_in,
    state_out, surface_out,
    span_row, sunlit, span_map, absorb, weights,
    state, partial, coupling, gain, depth, path, sun, packed, sky, flux, fluxes,
    in_sem, small_sem, out_sem, sky_send, sky_recv, pass_send, pass_recv, send_sem, recv_sem,
):
    fields, levels, blocks, _ = partial.shape
    bands = absorb.shape[0]
    chips = count // 2
    if count > 1:
        greet(count, "inface")
    small = [
        pltpu.make_async_copy(source, target, small_sem.at[i])
        for i, (source, target) in enumerate(
            [
                (cosine_in, packed.at[pl.ds(0, blocks)]),
                (albedo_in, packed.at[pl.ds(blocks, blocks)]),
                (sunlit_in, sunlit),
                (span_map_in, span_map),
                (span_map_in, span_row),
                (absorb_in, absorb),
                (weights_in, weights),
            ]
        )
    ]
    for copy in small:
        copy.start()
    me = lax.axis_index("inface") if count > 1 else 0

    def columns(c):
        return pl.ds(c * LANES, LANES)

    def field(f, first=0, size=blocks):
        return pl.ds(first * fields + f, size, stride=fields)

    for c in range(blocks):
        pltpu.make_async_copy(coupling_in.at[:, columns(c)], coupling.at[:, c, :], in_sem.at[0]).start()
    for c in range(blocks):
        pltpu.make_async_copy(state_in.at[:, :, columns(c)], state.at[:, pl.ds(c * fields, fields), :], in_sem.at[1]).start()

    for copy in small:
        copy.wait()
    for s in range(blocks):
        packed[pl.ds(s, 1), :] = packed[pl.ds(s, 1), :] * sunlit[0, s].astype(jnp.float32)
    flux[pl.ds(blocks, 8), :] = jnp.full((8, LANES), -1.0, jnp.float32)
    flux[pl.ds(blocks, 1), pl.ds(0, blocks)] = span_row[...].astype(jnp.float32)
    sky[me] = packed[...]
    sky_copies = []
    if count > 1:
        greeted(count)
        sibling = me + 1 - 2 * lax.rem(me, 2)
        for k in range(1, chips):
            peer = lax.rem(me + 2 * k, count)
            sky_copies.append(sky_copy("inface", packed, sky, me, peer, sky_send, sky_recv, k))
        sky_copies.append(sky_copy("inface", packed, sky, me, sibling, sky_send, sky_recv, 0))
        for copy in sky_copies:
            copy.start()

    pltpu.make_async_copy(coupling, coupling, in_sem.at[0]).wait()
    pltpu.make_async_copy(state, state, in_sem.at[1]).wait()

    if "solve" not in SKIP:
        below = coupling[0]
        scale = 1.0 / (1.0 + below)
        gain_now = below * scale
        gain[0] = gain_now
        values = []
        for f in range(fields):
            value = state[0, field(f), :] * scale
            partial[f, 0] = value
            values.append(value)

        def eliminate(l, carry):
            above, gain_last, *last = carry
            below = coupling[l]
            scale = 1.0 / (1.0 + below + above - above * gain_last)
            gain_now = below * scale
            gain[l] = gain_now
            now = []
            for f in range(fields):
                value = (state[l, field(f), :] + above * last[f]) * scale
                partial[f, l] = value
                now.append(value)
            return (below, gain_now, *now)

        carry = lax.fori_loop(1, levels, eliminate, (below, gain_now, *values), unroll=3)
        for f in range(fields):
            state[levels - 1, field(f), :] = carry[2 + f]

        def substitute(k, carry):
            l = levels - 2 - k
            g = gain[l]
            now = []
            for f in range(fields):
                value = partial[f, l] + g * carry[f]
                state[l, field(f), :] = value
                now.append(value)
            return tuple(now)

        lax.fori_loop(0, levels - 1, substitute, tuple(carry[2:]), unroll=3)

    if count > 1:
        for k in range(1, chips):
            origin = lax.rem(me + count - 2 * k, count)
            sky_copy("inface", packed, sky, origin, origin, sky_send, sky_recv, k).wait_recv()
            copy = sky_copy("inface", sky.at[origin], sky, origin, sibling, pass_send, pass_recv, k)
            copy.start()
            sky_copies.append(copy)

    def optics(l, nothing):
        depth[l] = 1.2 + jnp.tanh(state[l, field(1), :])
        return nothing

    lax.fori_loop(0, levels, optics, 0, unroll=2)

    if count > 1:
        sky_copy("inface", packed, sky, sibling, sibling, sky_send, sky_recv, 0).wait_recv()
        for k in range(1, chips):
            origin = lax.rem(sibling + count - 2 * k, count)
            sky_copy("inface", packed, sky, origin, sibling, pass_send, pass_recv, k).wait_recv()
        for copy in sky_copies:
            copy.wait_send()
    for e in range(blocks):
        span = span_map[0, e]
        owner, slot = span // blocks, span % blocks
        sun[0, pl.ds(e, 1), :] = sky[owner, pl.ds(slot, 1), :]
        sun[1, pl.ds(e, 1), :] = sky[owner, pl.ds(slot + blocks, 1), :]

    cosine_here = sun[0]
    slant = (-math.log2(math.e)) / jnp.where(cosine_here > 0.0, cosine_here, 1.0)

    def descend(l, total):
        step = depth[l] * slant
        depth[l] = step
        path[l] = total
        return total + step

    path[levels] = lax.fori_loop(0, levels, descend, jnp.zeros_like(slant), unroll=2)

    shape = (8, LANES)
    for g in range(blocks // 8):
        rows = pl.ds(g * 8, 8)
        total = jnp.zeros(shape, jnp.float32)
        for b in range(bands):
            total = total + weights[b] * jnp.exp2(absorb[b] * path[levels, rows, :])
        flux[rows, :] = (1.0 - sun[1, rows, :]) * sun[0, rows, :] * total
    fluxes[me] = flux[...]
    flux_copies = exchange(count, "inface", flux, fluxes, send_sem, recv_sem) if count > 1 else []

    for g in range(blocks // 8):
        rows = pl.ds(g * 8, 8)
        coefficient = [jnp.full(shape, absorb[b], jnp.float32) for b in range(bands)]
        weight = [jnp.full(shape, 0.3 * weights[b], jnp.float32) for b in range(bands)]
        reflected = sun[1, rows, :] * (1.0 / 0.3)
        low = path[levels, rows, :]
        ups = []
        sum_up = jnp.zeros(shape, jnp.float32)
        sum_down = jnp.zeros(shape, jnp.float32)
        for b in range(bands):
            down = weight[b] * jnp.exp2(coefficient[b] * low)
            up = reflected * down
            ups.append(up)
            sum_up = sum_up + up
            sum_down = sum_down + down
        net = sum_up - sum_down * (1.0 / 0.3)
        factor = 5.0 * sun[0, rows, :]

        def radiate(k, carry):
            l = levels - 1 - k
            net_below, *ups = carry
            step = depth[l, rows, :]
            above = path[l, rows, :]
            sum_up = [None, None]
            sum_down = [None, None]
            now = []
            for b in range(bands):
                passed = jnp.exp2(coefficient[b] * step)
                down = weight[b] * jnp.exp2(coefficient[b] * above)
                up = (ups[b] - down) * passed + down
                now.append(up)
                h = b % 2
                sum_up[h] = up if sum_up[h] is None else sum_up[h] + up
                sum_down[h] = down if sum_down[h] is None else sum_down[h] + down
            net = (sum_up[0] + sum_up[1]) - (sum_down[0] + sum_down[1]) * (1.0 / 0.3)
            here = field(0, g * 8, 8)
            state[l, here, :] = state[l, here, :] + factor * (net_below - net)
            return (net, *now)

        if "radiate" not in SKIP:
            lax.fori_loop(0, levels, radiate, (net, *ups), unroll=2)
        for c in range(g * 8, g * 8 + 8):
            pltpu.make_async_copy(state.at[:, pl.ds(c * fields, fields), :], state_out.at[:, :, columns(c)], out_sem.at[0]).start()

    if count > 1:
        finish(count, "inface", flux, fluxes, send_sem, recv_sem, flux_copies)
    mine = (lax.broadcasted_iota(jnp.int32, (blocks, blocks), 0) + me * blocks).astype(jnp.float32)
    surface = jnp.zeros((blocks, LANES), jnp.float32)
    for r in range(count):
        span_of = fluxes[r, pl.ds(blocks, 1), pl.ds(0, blocks)]
        pick = jnp.where(mine == span_of, 1.0, 0.0)
        surface = surface + jnp.dot(
            pick, fluxes[r, pl.ds(0, blocks), :], preferred_element_type=jnp.float32, precision=lax.Precision.HIGHEST
        )
    surface_out[...] = surface
    pltpu.make_async_copy(state, state, out_sem.at[0]).wait()


def run_step(count, cosine, albedo, sunlit, span_map, absorb, weights, model_state, coupling):
    levels, fields, columns = model_state.shape
    blocks = columns // LANES
    operands = (cosine, albedo, sunlit, span_map, absorb, weights, model_state, coupling)
    vmem = pl.BlockSpec(memory_space=pltpu.VMEM)
    anywhere = pl.BlockSpec(memory_space=pl.ANY)
    return pl.pallas_call(
        functools.partial(step_kernel, count),
        out_shape=(
            jax.ShapeDtypeStruct(model_state.shape, jnp.float32),
            jax.ShapeDtypeStruct((blocks, LANES), jnp.float32),
        ),
        in_specs=[pl.BlockSpec(memory_space=pltpu.HBM)] * 8,
        out_specs=(anywhere, vmem),
        scratch_shapes=[
            pltpu.VMEM(span_map.shape, jnp.int32),
            pltpu.SMEM(sunlit.shape, jnp.int32),
            pltpu.SMEM(span_map.shape, jnp.int32),
            pltpu.SMEM(absorb.shape, jnp.float32),
            pltpu.SMEM(weights.shape, jnp.float32),
            pltpu.VMEM((levels, blocks * fields, LANES), jnp.float32),
            pltpu.VMEM((fields, levels, blocks, LANES), jnp.float32),
            pltpu.VMEM((levels, blocks, LANES), jnp.float32),
            pltpu.VMEM((levels, blocks, LANES), jnp.float32),
            pltpu.VMEM((levels, blocks, LANES), jnp.float32),
            pltpu.VMEM((levels + 1, blocks, LANES), jnp.float32),
            pltpu.VMEM((2, blocks, LANES), jnp.float32),
            pltpu.VMEM((2 * blocks, LANES), jnp.float32),
            pltpu.VMEM((count, 2 * blocks, LANES), jnp.float32),
            pltpu.VMEM((blocks + 8, LANES), jnp.float32),
            pltpu.VMEM((count, blocks + 8, LANES), jnp.float32),
            pltpu.SemaphoreType.DMA((2,)),
            pltpu.SemaphoreType.DMA((7,)),
            pltpu.SemaphoreType.DMA((1,)),
            pltpu.SemaphoreType.DMA((max(count // 2, 1),)),
            pltpu.SemaphoreType.DMA((max(count // 2, 1),)),
            pltpu.SemaphoreType.DMA((max(count // 2, 1),)),
            pltpu.SemaphoreType.DMA((max(count // 2, 1),)),
            pltpu.SemaphoreType.DMA((count,)),
            pltpu.SemaphoreType.DMA((count,)),
        ],
        compiler_params=pltpu.CompilerParams(
            collective_id=0 if count > 1 else None, has_side_effects=True, vmem_limit_bytes=40 * 1024 * 1024
        ),
        name="step",
    )(*(pltpu.with_memory_space_constraint(x, pltpu.HBM) for x in operands))


def body(model_state, coupling, cosine, albedo, absorb, weights, span_map, sunlit):
    count = lax.axis_size("inface")
    spans = span_map.shape[1]
    new_state, surface = run_step(
        count,
        cosine.reshape(spans, LANES),
        albedo.reshape(spans, LANES),
        sunlit,
        span_map,
        absorb,
        weights,
        model_state.transpose(1, 0, 2),
        coupling,
    )
    return new_state.transpose(1, 0, 2), surface.reshape(cosine.shape)


def solution(mesh):
    in_specs = (
        P(None, None, ("face", "inface")),
        P(None, ("face", "inface")),
        P(("face", "inface")),
        P(("face", "inface")),
        P(),
        P(),
        P("face", "inface"),
        P("face", "inface"),
    )
    out_specs = (P(None, None, ("face", "inface")), P(("face", "inface")))
    return jax.shard_map(body, mesh=mesh, in_specs=in_specs, out_specs=out_specs, check_vma=False)
```

```python
import functools
import math

import jax
import jax.numpy as jnp
from jax import lax
from jax.experimental import pallas as pl
from jax.experimental.pallas import tpu as pltpu
from jax.sharding import PartitionSpec as P

MESH = pl.DeviceIdType.MESH
LANES = 128


def exchange(count, axis, source, target, send_sem, recv_sem):
    me = lax.axis_index(axis)
    copies = []
    for k in range(1, count):
        peer = lax.rem(me + k, count)
        copy = pltpu.make_async_remote_copy(
            src_ref=source,
            dst_ref=target.at[me],
            send_sem=send_sem.at[k],
            recv_sem=recv_sem.at[k],
            device_id={axis: peer},
            device_id_type=MESH,
        )
        copy.start()
        copies.append(copy)
    return copies


def finish(count, axis, source, target, send_sem, recv_sem, copies):
    me = lax.axis_index(axis)
    for k in range(1, count):
        origin = lax.rem(me + count - k, count)
        pltpu.make_async_remote_copy(
            src_ref=source,
            dst_ref=target.at[origin],
            send_sem=send_sem.at[k],
            recv_sem=recv_sem.at[k],
            device_id={axis: origin},
            device_id_type=MESH,
        ).wait_recv()
    for copy in copies:
        copy.wait_send()


def greet(count, axis):
    me = lax.axis_index(axis)
    barrier = pltpu.get_barrier_semaphore()
    for k in range(1, count):
        pl.semaphore_signal(barrier, inc=1, device_id={axis: lax.rem(me + k, count)}, device_id_type=MESH)


def greeted(count):
    pl.semaphore_wait(pltpu.get_barrier_semaphore(), count - 1)


def sky_copy(axis, source, target, owner, peer, send_sem, recv_sem, k):
    return pltpu.make_async_remote_copy(
        src_ref=source,
        dst_ref=target.at[owner],
        send_sem=send_sem.at[k],
        recv_sem=recv_sem.at[k],
        device_id={axis: peer},
        device_id_type=MESH,
    )


def step_kernel(
    count, cosine_in, albedo_in, sunlit_in, span_map_in, absorb_in, weights_in, state_in, coupling_in,
    state_out, surface_out,
    span_row, sunlit, span_map, absorb, weights,
    state, partial, coupling, gain, depth, path, sun, packed, sky, flux, fluxes,
    in_sem, small_sem, out_sem, sky_send, sky_recv, pass_send, pass_recv, send_sem, recv_sem,
):
    fields, levels, blocks, _ = partial.shape
    bands = absorb.shape[0]
    chips = count // 2
    if count > 1:
        greet(count, "inface")
    small = [
        pltpu.make_async_copy(source, target, small_sem.at[i])
        for i, (source, target) in enumerate(
            [
                (cosine_in, packed.at[pl.ds(0, blocks)]),
                (albedo_in, packed.at[pl.ds(blocks, blocks)]),
                (sunlit_in, sunlit),
                (span_map_in, span_map),
                (span_map_in, span_row),
                (absorb_in, absorb),
                (weights_in, weights),
            ]
        )
    ]
    for copy in small:
        copy.start()
    me = lax.axis_index("inface") if count > 1 else 0

    def columns(c):
        return pl.ds(c * LANES, LANES)

    def field(f, first=0, size=blocks):
        return pl.ds(first * fields + f, size, stride=fields)

    for copy in small:
        copy.wait()
    for s in range(blocks):
        packed[pl.ds(s, 1), :] = packed[pl.ds(s, 1), :] * sunlit[0, s].astype(jnp.float32)
    flux[pl.ds(blocks, 8), :] = jnp.full((8, LANES), -1.0, jnp.float32)
    flux[pl.ds(blocks, 1), pl.ds(0, blocks)] = span_row[...].astype(jnp.float32)
    sky[me] = packed[...]
    sky_copies = []
    if count > 1:
        greeted(count)
        sibling = me + 1 - 2 * lax.rem(me, 2)
        for k in range(1, chips):
            peer = lax.rem(me + 2 * k, count)
            sky_copies.append(sky_copy("inface", packed, sky, me, peer, sky_send, sky_recv, k))
        sky_copies.append(sky_copy("inface", packed, sky, me, sibling, sky_send, sky_recv, 0))
        for copy in sky_copies:
            copy.start()

    for c in range(blocks):
        pltpu.make_async_copy(coupling_in.at[:, columns(c)], coupling.at[:, c, :], in_sem.at[0]).start()
    for c in range(blocks):
        pltpu.make_async_copy(state_in.at[:, :, columns(c)], state.at[:, pl.ds(c * fields, fields), :], in_sem.at[1]).start()

    pltpu.make_async_copy(coupling, coupling, in_sem.at[0]).wait()
    pltpu.make_async_copy(state, state, in_sem.at[1]).wait()

    below = coupling[0]
    scale = 1.0 / (1.0 + below)
    gain_now = below * scale
    gain[0] = gain_now
    values = []
    for f in range(fields):
        value = state[0, field(f), :] * scale
        partial[f, 0] = value
        values.append(value)

    def eliminate(l, carry):
        above, gain_last, *last = carry
        below = coupling[l]
        scale = 1.0 / (1.0 + below + above - above * gain_last)
        gain_now = below * scale
        gain[l] = gain_now
        now = []
        for f in range(fields):
            value = (state[l, field(f), :] + above * last[f]) * scale
            partial[f, l] = value
            now.append(value)
        return (below, gain_now, *now)

    carry = lax.fori_loop(1, levels, eliminate, (below, gain_now, *values), unroll=8)
    for f in range(fields):
        state[levels - 1, field(f), :] = carry[2 + f]

    def substitute(k, carry):
        l = levels - 2 - k
        g = gain[l]
        now = []
        for f in range(fields):
            value = partial[f, l] + g * carry[f]
            state[l, field(f), :] = value
            now.append(value)
        return tuple(now)

    lax.fori_loop(0, levels - 1, substitute, tuple(carry[2:]), unroll=8)

    if count > 1:
        for k in range(1, chips):
            origin = lax.rem(me + count - 2 * k, count)
            sky_copy("inface", packed, sky, origin, origin, sky_send, sky_recv, k).wait_recv()
            copy = sky_copy("inface", sky.at[origin], sky, origin, sibling, pass_send, pass_recv, k)
            copy.start()
            sky_copies.append(copy)

    def optics(l, nothing):
        depth[l] = 1.2 + jnp.tanh(state[l, field(1), :])
        return nothing

    lax.fori_loop(0, levels, optics, 0, unroll=8)

    if count > 1:
        sky_copy("inface", packed, sky, sibling, sibling, sky_send, sky_recv, 0).wait_recv()
        for k in range(1, chips):
            origin = lax.rem(sibling + count - 2 * k, count)
            sky_copy("inface", packed, sky, origin, sibling, pass_send, pass_recv, k).wait_recv()
        for copy in sky_copies:
            copy.wait_send()
    for e in range(blocks):
        span = span_map[0, e]
        owner, slot = span // blocks, span % blocks
        sun[0, pl.ds(e, 1), :] = sky[owner, pl.ds(slot, 1), :]
        sun[1, pl.ds(e, 1), :] = sky[owner, pl.ds(slot + blocks, 1), :]

    cosine_here = sun[0]
    slant = (-math.log2(math.e)) / jnp.where(cosine_here > 0.0, cosine_here, 1.0)

    def descend(l, total):
        step = depth[l] * slant
        depth[l] = step
        path[l] = total
        return total + step

    path[levels] = lax.fori_loop(0, levels, descend, jnp.zeros_like(slant), unroll=8)

    shape = (8, LANES)
    for g in range(blocks // 8):
        rows = pl.ds(g * 8, 8)
        total = jnp.zeros(shape, jnp.float32)
        for b in range(bands):
            total = total + weights[b] * jnp.exp2(absorb[b] * path[levels, rows, :])
        flux[rows, :] = (1.0 - sun[1, rows, :]) * sun[0, rows, :] * total
    fluxes[me] = flux[...]
    flux_copies = exchange(count, "inface", flux, fluxes, send_sem, recv_sem) if count > 1 else []

    for g in range(blocks // 8):
        rows = pl.ds(g * 8, 8)
        coefficient = [jnp.full(shape, absorb[b], jnp.float32) for b in range(bands)]
        weight = [jnp.full(shape, 0.3 * weights[b], jnp.float32) for b in range(bands)]
        reflected = sun[1, rows, :] * (1.0 / 0.3)
        low = path[levels, rows, :]
        ups = []
        sum_up = jnp.zeros(shape, jnp.float32)
        sum_down = jnp.zeros(shape, jnp.float32)
        for b in range(bands):
            down = weight[b] * jnp.exp2(coefficient[b] * low)
            up = reflected * down
            ups.append(up)
            sum_up = sum_up + up
            sum_down = sum_down + down
        net = sum_up - sum_down * (1.0 / 0.3)
        factor = 5.0 * sun[0, rows, :]

        def radiate(k, carry):
            l = levels - 1 - k
            net_below, *ups = carry
            step = depth[l, rows, :]
            above = path[l, rows, :]
            sum_up = [None, None]
            sum_down = [None, None]
            now = []
            for b in range(bands):
                passed = jnp.exp2(coefficient[b] * step)
                down = weight[b] * jnp.exp2(coefficient[b] * above)
                up = (ups[b] - down) * passed + down
                now.append(up)
                h = b % 2
                sum_up[h] = up if sum_up[h] is None else sum_up[h] + up
                sum_down[h] = down if sum_down[h] is None else sum_down[h] + down
            net = (sum_up[0] + sum_up[1]) - (sum_down[0] + sum_down[1]) * (1.0 / 0.3)
            here = field(0, g * 8, 8)
            state[l, here, :] = state[l, here, :] + factor * (net_below - net)
            return (net, *now)

        lax.fori_loop(0, levels, radiate, (net, *ups), unroll=29)
        for c in range(g * 8, g * 8 + 8):
            pltpu.make_async_copy(state.at[:, pl.ds(c * fields, fields), :], state_out.at[:, :, columns(c)], out_sem.at[0]).start()

    if count > 1:
        finish(count, "inface", flux, fluxes, send_sem, recv_sem, flux_copies)
    mine = (lax.broadcasted_iota(jnp.int32, (blocks, count * blocks), 0) + me * blocks).astype(jnp.float32)
    span_of = jnp.concatenate([fluxes[r, pl.ds(blocks, 1), pl.ds(0, blocks)] for r in range(count)], axis=1)
    every = jnp.concatenate([fluxes[r, pl.ds(0, blocks), :] for r in range(count)], axis=0)
    surface = jnp.dot(
        jnp.where(mine == span_of, 1.0, 0.0),
        every,
        preferred_element_type=jnp.float32,
        precision=lax.Precision.HIGHEST,
    )
    surface_out[...] = surface
    pltpu.make_async_copy(state, state, out_sem.at[0]).wait()


def run_step(count, cosine, albedo, sunlit, span_map, absorb, weights, model_state, coupling):
    levels, fields, columns = model_state.shape
    blocks = columns // LANES
    operands = (cosine, albedo, sunlit, span_map, absorb, weights, model_state, coupling)
    vmem = pl.BlockSpec(memory_space=pltpu.VMEM)
    anywhere = pl.BlockSpec(memory_space=pl.ANY)
    return pl.pallas_call(
        functools.partial(step_kernel, count),
        out_shape=(
            jax.ShapeDtypeStruct(model_state.shape, jnp.float32),
            jax.ShapeDtypeStruct((blocks, LANES), jnp.float32),
        ),
        in_specs=[pl.BlockSpec(memory_space=pltpu.HBM)] * 8,
        out_specs=(anywhere, vmem),
        scratch_shapes=[
            pltpu.VMEM(span_map.shape, jnp.int32),
            pltpu.SMEM(sunlit.shape, jnp.int32),
            pltpu.SMEM(span_map.shape, jnp.int32),
            pltpu.SMEM(absorb.shape, jnp.float32),
            pltpu.SMEM(weights.shape, jnp.float32),
            pltpu.VMEM((levels, blocks * fields, LANES), jnp.float32),
            pltpu.VMEM((fields, levels, blocks, LANES), jnp.float32),
            pltpu.VMEM((levels, blocks, LANES), jnp.float32),
            pltpu.VMEM((levels, blocks, LANES), jnp.float32),
            pltpu.VMEM((levels, blocks, LANES), jnp.float32),
            pltpu.VMEM((levels + 1, blocks, LANES), jnp.float32),
            pltpu.VMEM((2, blocks, LANES), jnp.float32),
            pltpu.VMEM((2 * blocks, LANES), jnp.float32),
            pltpu.VMEM((count, 2 * blocks, LANES), jnp.float32),
            pltpu.VMEM((blocks + 8, LANES), jnp.float32),
            pltpu.VMEM((count, blocks + 8, LANES), jnp.float32),
            pltpu.SemaphoreType.DMA((2,)),
            pltpu.SemaphoreType.DMA((7,)),
            pltpu.SemaphoreType.DMA((1,)),
            pltpu.SemaphoreType.DMA((max(count // 2, 1),)),
            pltpu.SemaphoreType.DMA((max(count // 2, 1),)),
            pltpu.SemaphoreType.DMA((max(count // 2, 1),)),
            pltpu.SemaphoreType.DMA((max(count // 2, 1),)),
            pltpu.SemaphoreType.DMA((count,)),
            pltpu.SemaphoreType.DMA((count,)),
        ],
        compiler_params=pltpu.CompilerParams(
            collective_id=0 if count > 1 else None, has_side_effects=True, vmem_limit_bytes=40 * 1024 * 1024
        ),
        name="step",
    )(*(pltpu.with_memory_space_constraint(x, pltpu.HBM) for x in operands))


def body(model_state, coupling, cosine, albedo, absorb, weights, span_map, sunlit):
    count = lax.axis_size("inface")
    spans = span_map.shape[1]
    new_state, surface = run_step(
        count,
        cosine.reshape(spans, LANES),
        albedo.reshape(spans, LANES),
        sunlit,
        span_map,
        absorb,
        weights,
        model_state.transpose(1, 0, 2),
        coupling,
    )
    return new_state.transpose(1, 0, 2), surface.reshape(cosine.shape)


def solution(mesh):
    in_specs = (
        P(None, None, ("face", "inface")),
        P(None, ("face", "inface")),
        P(("face", "inface")),
        P(("face", "inface")),
        P(),
        P(),
        P("face", "inface"),
        P("face", "inface"),
    )
    out_specs = (P(None, None, ("face", "inface")), P(("face", "inface")))
    return jax.shard_map(body, mesh=mesh, in_specs=in_specs, out_specs=out_specs, check_vma=False)
```

```python
import functools
import math

import jax
import jax.numpy as jnp
from jax import lax
from jax.experimental import pallas as pl
from jax.experimental.pallas import tpu as pltpu
from jax.sharding import PartitionSpec as P

MESH = pl.DeviceIdType.MESH
LANES = 128


def exchange(count, axis, source, target, send_sem, recv_sem):
    me = lax.axis_index(axis)
    copies = []
    for k in range(1, count):
        peer = lax.rem(me + k, count)
        copy = pltpu.make_async_remote_copy(
            src_ref=source,
            dst_ref=target.at[me],
            send_sem=send_sem.at[k],
            recv_sem=recv_sem.at[k],
            device_id={axis: peer},
            device_id_type=MESH,
        )
        copy.start()
        copies.append(copy)
    return copies


def finish(count, axis, source, target, send_sem, recv_sem, copies):
    me = lax.axis_index(axis)
    for k in range(1, count):
        origin = lax.rem(me + count - k, count)
        pltpu.make_async_remote_copy(
            src_ref=source,
            dst_ref=target.at[origin],
            send_sem=send_sem.at[k],
            recv_sem=recv_sem.at[k],
            device_id={axis: origin},
            device_id_type=MESH,
        ).wait_recv()
    for copy in copies:
        copy.wait_send()


def greet(count, axis):
    me = lax.axis_index(axis)
    barrier = pltpu.get_barrier_semaphore()
    for k in range(1, count):
        pl.semaphore_signal(barrier, inc=1, device_id={axis: lax.rem(me + k, count)}, device_id_type=MESH)


def greeted(count):
    pl.semaphore_wait(pltpu.get_barrier_semaphore(), count - 1)


def sky_copy(axis, source, target, owner, peer, send_sem, recv_sem, k):
    return pltpu.make_async_remote_copy(
        src_ref=source,
        dst_ref=target.at[owner],
        send_sem=send_sem.at[k],
        recv_sem=recv_sem.at[k],
        device_id={axis: peer},
        device_id_type=MESH,
    )


def step_kernel(
    count, cosine_in, albedo_in, sunlit_in, span_map_in, absorb_in, weights_in, state_in, coupling_in,
    state_out, surface_out,
    span_row, sunlit, span_map, absorb, weights,
    state, partial, coupling, gain, depth, path, sun, packed, sky, flux, fluxes,
    in_sem, small_sem, out_sem, sky_send, sky_recv, pass_send, pass_recv, send_sem, recv_sem,
):
    fields, levels, blocks, _ = partial.shape
    bands = absorb.shape[0]
    chips = count // 2
    if count > 1:
        greet(count, "inface")
    small = [
        pltpu.make_async_copy(source, target, small_sem.at[i])
        for i, (source, target) in enumerate(
            [
                (cosine_in, packed.at[pl.ds(0, blocks)]),
                (albedo_in, packed.at[pl.ds(blocks, blocks)]),
                (sunlit_in, sunlit),
                (span_map_in, span_map),
                (span_map_in, span_row),
                (absorb_in, absorb),
                (weights_in, weights),
            ]
        )
    ]
    for copy in small:
        copy.start()
    me = lax.axis_index("inface") if count > 1 else 0

    def columns(c):
        return pl.ds(c * LANES, LANES)

    def field(f, first=0, size=blocks):
        return pl.ds(first * fields + f, size, stride=fields)

    for c in range(blocks):
        pltpu.make_async_copy(coupling_in.at[:, columns(c)], coupling.at[:, c, :], in_sem.at[0]).start()
    for c in range(blocks):
        pltpu.make_async_copy(state_in.at[:, :, columns(c)], state.at[:, pl.ds(c * fields, fields), :], in_sem.at[1]).start()

    for copy in small:
        copy.wait()
    for s in range(blocks):
        packed[pl.ds(s, 1), :] = packed[pl.ds(s, 1), :] * sunlit[0, s].astype(jnp.float32)
    flux[pl.ds(blocks, 8), :] = jnp.full((8, LANES), -1.0, jnp.float32)
    flux[pl.ds(blocks, 1), pl.ds(0, blocks)] = span_row[...].astype(jnp.float32)
    sky[me] = packed[...]
    sky_copies = []
    if count > 1:
        greeted(count)
        sibling = me + 1 - 2 * lax.rem(me, 2)
        for k in range(1, chips):
            peer = lax.rem(me + 2 * k, count)
            sky_copies.append(sky_copy("inface", packed, sky, me, peer, sky_send, sky_recv, k))
        sky_copies.append(sky_copy("inface", packed, sky, me, sibling, sky_send, sky_recv, 0))
        for copy in sky_copies:
            copy.start()

    pltpu.make_async_copy(coupling, coupling, in_sem.at[0]).wait()
    pltpu.make_async_copy(state, state, in_sem.at[1]).wait()

    below = coupling[0]
    scale = 1.0 / (1.0 + below)
    gain_now = below * scale
    gain[0] = gain_now
    values = []
    for f in range(fields):
        value = state[0, field(f), :] * scale
        partial[f, 0] = value
        values.append(value)

    def eliminate(l, carry):
        above, gain_last, *last = carry
        below = coupling[l]
        scale = 1.0 / (1.0 + below + above - above * gain_last)
        gain_now = below * scale
        gain[l] = gain_now
        now = []
        for f in range(fields):
            value = (state[l, field(f), :] + above * last[f]) * scale
            partial[f, l] = value
            now.append(value)
        return (below, gain_now, *now)

    carry = lax.fori_loop(1, levels, eliminate, (below, gain_now, *values), unroll=8)
    for f in range(fields):
        state[levels - 1, field(f), :] = carry[2 + f]

    def substitute(k, carry):
        l = levels - 2 - k
        g = gain[l]
        now = []
        for f in range(fields):
            value = partial[f, l] + g * carry[f]
            state[l, field(f), :] = value
            now.append(value)
        return tuple(now)

    lax.fori_loop(0, levels - 1, substitute, tuple(carry[2:]), unroll=8)

    if count > 1:
        for k in range(1, chips):
            origin = lax.rem(me + count - 2 * k, count)
            sky_copy("inface", packed, sky, origin, origin, sky_send, sky_recv, k).wait_recv()
            copy = sky_copy("inface", sky.at[origin], sky, origin, sibling, pass_send, pass_recv, k)
            copy.start()
            sky_copies.append(copy)

    def optics(l, nothing):
        depth[l] = 1.2 + jnp.tanh(state[l, field(1), :])
        return nothing

    lax.fori_loop(0, levels, optics, 0, unroll=8)

    if count > 1:
        sky_copy("inface", packed, sky, sibling, sibling, sky_send, sky_recv, 0).wait_recv()
        for k in range(1, chips):
            origin = lax.rem(sibling + count - 2 * k, count)
            sky_copy("inface", packed, sky, origin, sibling, pass_send, pass_recv, k).wait_recv()
        for copy in sky_copies:
            copy.wait_send()
    for e in range(blocks):
        span = span_map[0, e]
        owner, slot = span // blocks, span % blocks
        sun[0, pl.ds(e, 1), :] = sky[owner, pl.ds(slot, 1), :]
        sun[1, pl.ds(e, 1), :] = sky[owner, pl.ds(slot + blocks, 1), :]

    cosine_here = sun[0]
    slant = (-math.log2(math.e)) / jnp.where(cosine_here > 0.0, cosine_here, 1.0)

    def descend(l, total):
        step = depth[l] * slant
        depth[l] = step
        path[l] = total
        return total + step

    path[levels] = lax.fori_loop(0, levels, descend, jnp.zeros_like(slant), unroll=8)

    shape = (8, LANES)
    for g in range(blocks // 8):
        rows = pl.ds(g * 8, 8)
        total = jnp.zeros(shape, jnp.float32)
        for b in range(bands):
            total = total + weights[b] * jnp.exp2(absorb[b] * path[levels, rows, :])
        flux[rows, :] = (1.0 - sun[1, rows, :]) * sun[0, rows, :] * total
    fluxes[me] = flux[...]
    flux_copies = exchange(count, "inface", flux, fluxes, send_sem, recv_sem) if count > 1 else []

    for g in range(blocks // 8):
        rows = pl.ds(g * 8, 8)
        coefficient = [jnp.full(shape, absorb[b], jnp.float32) for b in range(bands)]
        weight = [jnp.full(shape, 0.3 * weights[b], jnp.float32) for b in range(bands)]
        reflected = sun[1, rows, :] * (1.0 / 0.3)
        low = path[levels, rows, :]
        ups = []
        sum_up = jnp.zeros(shape, jnp.float32)
        sum_down = jnp.zeros(shape, jnp.float32)
        for b in range(bands):
            down = weight[b] * jnp.exp2(coefficient[b] * low)
            up = reflected * down
            ups.append(up)
            sum_up = sum_up + up
            sum_down = sum_down + down
        net = sum_up - sum_down * (1.0 / 0.3)
        factor = 5.0 * sun[0, rows, :]

        def radiate(k, carry):
            l = levels - 1 - k
            net_below, *ups = carry
            step = depth[l, rows, :]
            above = path[l, rows, :]
            sum_up = [None, None]
            sum_down = [None, None]
            now = []
            for b in range(bands):
                passed = jnp.exp2(coefficient[b] * step)
                down = weight[b] * jnp.exp2(coefficient[b] * above)
                up = (ups[b] - down) * passed + down
                now.append(up)
                h = b % 2
                sum_up[h] = up if sum_up[h] is None else sum_up[h] + up
                sum_down[h] = down if sum_down[h] is None else sum_down[h] + down
            net = (sum_up[0] + sum_up[1]) - (sum_down[0] + sum_down[1]) * (1.0 / 0.3)
            here = field(0, g * 8, 8)
            state[l, here, :] = state[l, here, :] + factor * (net_below - net)
            return (net, *now)

        lax.fori_loop(0, levels, radiate, (net, *ups), unroll=29)
        for c in range(g * 8, g * 8 + 8):
            pltpu.make_async_copy(state.at[:, pl.ds(c * fields, fields), :], state_out.at[:, :, columns(c)], out_sem.at[0]).start()

    if count > 1:
        finish(count, "inface", flux, fluxes, send_sem, recv_sem, flux_copies)
    mine = (lax.broadcasted_iota(jnp.int32, (blocks, count * blocks), 0) + me * blocks).astype(jnp.float32)
    span_of = jnp.concatenate([fluxes[r, pl.ds(blocks, 1), pl.ds(0, blocks)] for r in range(count)], axis=1)
    every = jnp.concatenate([fluxes[r, pl.ds(0, blocks), :] for r in range(count)], axis=0)
    surface = jnp.dot(
        jnp.where(mine == span_of, 1.0, 0.0),
        every,
        preferred_element_type=jnp.float32,
        precision=lax.Precision.HIGHEST,
    )
    surface_out[...] = surface
    pltpu.make_async_copy(state, state, out_sem.at[0]).wait()


def run_step(count, cosine, albedo, sunlit, span_map, absorb, weights, model_state, coupling):
    levels, fields, columns = model_state.shape
    blocks = columns // LANES
    operands = (cosine, albedo, sunlit, span_map, absorb, weights, model_state, coupling)
    vmem = pl.BlockSpec(memory_space=pltpu.VMEM)
    anywhere = pl.BlockSpec(memory_space=pl.ANY)
    return pl.pallas_call(
        functools.partial(step_kernel, count),
        out_shape=(
            jax.ShapeDtypeStruct(model_state.shape, jnp.float32),
            jax.ShapeDtypeStruct((blocks, LANES), jnp.float32),
        ),
        in_specs=[pl.BlockSpec(memory_space=pltpu.HBM)] * 8,
        out_specs=(anywhere, vmem),
        scratch_shapes=[
            pltpu.VMEM(span_map.shape, jnp.int32),
            pltpu.SMEM(sunlit.shape, jnp.int32),
            pltpu.SMEM(span_map.shape, jnp.int32),
            pltpu.SMEM(absorb.shape, jnp.float32),
            pltpu.SMEM(weights.shape, jnp.float32),
            pltpu.VMEM((levels, blocks * fields, LANES), jnp.float32),
            pltpu.VMEM((fields, levels, blocks, LANES), jnp.float32),
            pltpu.VMEM((levels, blocks, LANES), jnp.float32),
            pltpu.VMEM((levels, blocks, LANES), jnp.float32),
            pltpu.VMEM((levels, blocks, LANES), jnp.float32),
            pltpu.VMEM((levels + 1, blocks, LANES), jnp.float32),
            pltpu.VMEM((2, blocks, LANES), jnp.float32),
            pltpu.VMEM((2 * blocks, LANES), jnp.float32),
            pltpu.VMEM((count, 2 * blocks, LANES), jnp.float32),
            pltpu.VMEM((blocks + 8, LANES), jnp.float32),
            pltpu.VMEM((count, blocks + 8, LANES), jnp.float32),
            pltpu.SemaphoreType.DMA((2,)),
            pltpu.SemaphoreType.DMA((7,)),
            pltpu.SemaphoreType.DMA((1,)),
            pltpu.SemaphoreType.DMA((max(count // 2, 1),)),
            pltpu.SemaphoreType.DMA((max(count // 2, 1),)),
            pltpu.SemaphoreType.DMA((max(count // 2, 1),)),
            pltpu.SemaphoreType.DMA((max(count // 2, 1),)),
            pltpu.SemaphoreType.DMA((count,)),
            pltpu.SemaphoreType.DMA((count,)),
        ],
        compiler_params=pltpu.CompilerParams(
            collective_id=0 if count > 1 else None, has_side_effects=True, vmem_limit_bytes=40 * 1024 * 1024
        ),
        name="step",
    )(*(pltpu.with_memory_space_constraint(x, pltpu.HBM) for x in operands))


def body(model_state, coupling, cosine, albedo, absorb, weights, span_map, sunlit):
    count = lax.axis_size("inface")
    spans = span_map.shape[1]
    new_state, surface = run_step(
        count,
        cosine.reshape(spans, LANES),
        albedo.reshape(spans, LANES),
        sunlit,
        span_map,
        absorb,
        weights,
        model_state.transpose(1, 0, 2),
        coupling,
    )
    return new_state.transpose(1, 0, 2), surface.reshape(cosine.shape)


def solution(mesh):
    in_specs = (
        P(None, None, ("face", "inface")),
        P(None, ("face", "inface")),
        P(("face", "inface")),
        P(("face", "inface")),
        P(),
        P(),
        P("face", "inface"),
        P("face", "inface"),
    )
    out_specs = (P(None, None, ("face", "inface")), P(("face", "inface")))
    return jax.shard_map(body, mesh=mesh, in_specs=in_specs, out_specs=out_specs, check_vma=False)
```
